512 devices in a mesh: dp: 16 (over x, y_lo), seq: 32 (over z, y_hi, core).
Axes of the slice: x: 4, y: 8 (y_hi: 2, y_lo: 4; y = y_hi * 4 + y_lo), z: 8, core: 2. Of those that a mesh axis runs over, the one named last changes fastest.
Arguments:
- inputs: bfloat16 [16, 16384, 1024], P('dp', 'seq'), may hold values from -6 to 6
- cotangent: bfloat16 [16, 16384, 1024], P('dp', 'seq'), may hold values from -6 to 6
- block_right: bfloat16 [32, 512, 512], P('seq'), may hold values from -0.25 to 0.25
- block_left: bfloat16 [512, 32, 32], P('seq'), may hold values from -1 to 1
- gate_in: float32 [1024], replicated, may hold values from 0.1 to 1.9
- gate_out: float32 [1024], replicated, may hold values from -3 to 3
Outputs:
- d_inputs: bfloat16 [16, 16384, 1024], P('dp', 'seq')
- d_right: float32 [32, 512, 512], P('seq')
- d_left: float32 [512, 32, 32], P('seq')
- d_gate_in: float32 [1024], replicated
- d_gate_out: float32 [1024], replicated
The draws below stay inside these ranges and needn't reach their ends.
All inputs are finite; a program needn't handle non-finite values.
Results may differ from the reference program's by a relative error of at most 0.006.
Values may be sent and summed in bfloat16 or wider, within the bound.
A program may use at most 64 MiB of HBM per device.

```python
import jax
import jax.numpy as jnp
from jax import lax

D = 1024
S2 = 512
S1 = 32
TOKENS = 16384
BATCH = 16


def shard_levels(rng, dims, pieces, smallest, top_value):
    loudness, own = 1.0, jax.random.fold_in(rng, 6)
    for position, parts in pieces:
        draws = jnp.exp(jax.random.uniform(jax.random.fold_in(own, position), (parts,), jnp.float32, smallest / len(pieces), top_value / len(pieces)))
        loudness = loudness * jnp.repeat(draws, dims[position] // parts).reshape([-1 if axis == position else 1 for axis in range(len(dims))])
    return loudness


def centred(rng, extent, deviation, limit, pieces=(), kind=jnp.bfloat16):
    values = jax.random.normal(rng, extent, jnp.float32) * deviation
    if len(pieces) > 0:
        values = shard_levels(rng, extent, pieces, -0.22, 0.18) * values
    return jnp.clip(values, min=-limit, max=limit).astype(kind)


def setup_inputs(seed: int = 0) -> dict:
    streams_of = jax.random.split(jax.random.key(seed), 7)
    inputs = centred(streams_of[0], (BATCH, TOKENS, D), 1.0, 6.0, ((0, 16), (1, 32)))
    cotangent = centred(streams_of[1], (BATCH, TOKENS, D), 1.0, 6.0, ((0, 16), (1, 32)))
    block_right = centred(streams_of[2], (S1, S2, S2), S2 ** -0.5, 0.25, ((0, 32),))
    block_left = centred(streams_of[3], (S2, S1, S1), S1 ** -0.5, 1.0, ((0, 32),))
    gate_in = jnp.clip(1.0 + 0.18 * jax.random.normal(streams_of[4], (D,), jnp.float32), 0.1, 1.9)
    gate_out = centred(streams_of[5], (D,), 1.0, 3.0, (), jnp.float32)
    return {"inputs": inputs, "cotangent": cotangent, "block_right": block_right, "block_left": block_left, "gate_in": gate_in, "gate_out": gate_out}


def reference(inputs, cotangent, block_right, block_left, gate_in, gate_out):
    right_wide = block_right.astype(jnp.float32)
    left_wide = block_left.astype(jnp.float32)

    def sample_step(carry, pair):
        sample_in, sample_cot = pair
        input_wide = sample_in.astype(jnp.float32).reshape(S1, S2, D)
        cot_wide = sample_cot.astype(jnp.float32).reshape(S1, S2, D)
        hidden = (input_wide * gate_in).astype(jnp.bfloat16)
        mixed = jnp.einsum('acb,abd->acd', right_wide, hidden.astype(jnp.float32)).astype(jnp.bfloat16)
        monarch = jnp.einsum('cea,acd->ecd', left_wide, mixed.astype(jnp.float32)).astype(jnp.bfloat16)
        monarch_wide = monarch.astype(jnp.float32)
        sig = jax.nn.sigmoid(input_wide * gate_out)
        d_monarch = (cot_wide * sig).astype(jnp.bfloat16)
        d_pre = cot_wide * monarch_wide * sig * (1.0 - sig)
        gate_grad = lax.optimization_barrier((d_pre * gate_out).astype(jnp.bfloat16)).astype(jnp.float32)
        d_mixed = jnp.einsum('cea,ecd->acd', left_wide, d_monarch.astype(jnp.float32)).astype(jnp.bfloat16)
        d_hidden = jnp.einsum('acb,acd->abd', right_wide, d_mixed.astype(jnp.float32))
        d_inputs = (gate_grad + d_hidden * gate_in).astype(jnp.bfloat16).reshape(TOKENS, D)
        term_right = jnp.einsum('acd,abd->acb', d_mixed.astype(jnp.float32), hidden.astype(jnp.float32))
        term_left = jnp.einsum('ecd,acd->cea', d_monarch.astype(jnp.float32), mixed.astype(jnp.float32))
        term_gin = lax.optimization_barrier(jnp.sum(d_hidden * input_wide, axis=(0, 1)))
        term_gout = lax.optimization_barrier(jnp.sum(d_pre * input_wide, axis=(0, 1)))
        sum_right, sum_left, sum_gin, sum_gout = carry
        return ((sum_right + term_right, sum_left + term_left, sum_gin + term_gin, sum_gout + term_gout), d_inputs)
    start = (jnp.zeros((S1, S2, S2), jnp.float32), jnp.zeros((S2, S1, S1), jnp.float32), jnp.zeros((D,), jnp.float32), jnp.zeros((D,), jnp.float32))
    totals, d_inputs = lax.scan(sample_step, start, (inputs, cotangent))
    factor_scale = 1.0 / jnp.sqrt(jnp.float32(BATCH * D))
    gate_scale = 1.0 / jnp.sqrt(jnp.float32(BATCH * TOKENS))
    return (d_inputs, totals[0] * factor_scale, totals[1] * factor_scale, totals[2] * gate_scale, totals[3] * gate_scale)
```

```python
import functools

import jax
import jax.numpy as jnp
from jax import lax
from jax.experimental import pallas as pl
from jax.experimental.pallas import tpu as pltpu
from jax.sharding import PartitionSpec as P

MESH = pl.DeviceIdType.MESH
F32 = jnp.float32
BF16 = jnp.bfloat16
K = 4
D = 1024
CH = D // K
N = 512
DMON, MIX, DMIX, MON = 0, 1, 2, 3
NT = (((1,), (1,)), ((), ()))


def dot(a, b):
    return jnp.dot(a, b, preferred_element_type=F32)


def dot_nt(a, b):
    return lax.dot_general(a, b, NT, preferred_element_type=F32)


def natural(p):
    return ((p // 2) % 8) * 4 + (p // 16) * 2 + p % 2


def iota(shape, dim):
    return lax.broadcasted_iota(jnp.int32, shape, dim)


def kernel(
    x_hbm, c_hbm, r_hbm, l_ref, gi_ref, go_ref,
    o_hbm, dr_hbm, dl_ref, dgi_ref, dgo_ref,
    xv, cv, hv, p1, dh, out, rr, rt, ww, wt,
    tbuf, sbuf, rbuf, racc, lacc, gacc,
    gxs, gxr, gys, gyr, fin, drv, lx, ly, ga, gb, gc,
    in_sem, out_sem, ys, yr, zs, zr, rs_s, rs_r, sm_s, sm_r,
):
    dp = lax.axis_index("dp")
    seq = lax.axis_index("seq")
    xx, yl = dp // 4, dp % 4
    z, yh, core = seq // 4, (seq // 2) % 2, seq % 2
    oth = 1 - yh
    me = z * 2 + core
    ring = yh * 4 + yl

    def zc_peer(q):
        return (dp, (q // 2) * 4 + yh * 2 + q % 2)

    def x_peer(q):
        return (q * 4 + yl, seq)

    def y_peer(q):
        return (xx * 4 + q % 4, z * 4 + (q // 4) * 2 + core)

    partner = (dp, z * 4 + oth * 2 + core)

    def load_x(k):
        return pltpu.make_async_copy(x_hbm.at[0, :, pl.ds(k * CH, CH)], xv.at[k], in_sem.at[k])

    def load_c(k):
        return pltpu.make_async_copy(c_hbm.at[0, :, pl.ds(k * CH, CH)], cv.at[k], in_sem.at[K + k])

    def load_r(h):
        return pltpu.make_async_copy(r_hbm.at[:, h], rr.at[h], in_sem.at[2 * K + h])

    for k in range(K):
        load_x(k).start()
        load_c(k).start()
    for h in range(2):
        load_r(h).start()

    barrier = pltpu.get_barrier_semaphore()

    def greet(peer_of, mine, n):
        def step(i, _):
            pl.semaphore_signal(
                barrier, inc=1, device_id=peer_of(lax.rem(mine + i, n)), device_id_type=MESH
            )
            return 0

        lax.fori_loop(1, n, step, 0)

    greet(zc_peer, me, 16)
    greet(x_peer, xx, 4)
    greet(y_peer, ring, 8)

    def y_copy(s):
        return pltpu.make_async_remote_copy(
            src_ref=tbuf.at[s],
            dst_ref=sbuf.at[s, yh],
            send_sem=ys.at[s],
            recv_sem=yr.at[s],
            device_id=partner,
            device_id_type=MESH,
        )

    def y_arrived(s):
        pltpu.make_async_copy(sbuf.at[s, oth], sbuf.at[s, oth], yr.at[s]).wait()

    def z_send(s):
        pltpu.make_async_copy(sbuf.at[s, :, me], rbuf.at[s, :, me], zr.at[s]).start()

        def step(i, _):
            q = lax.rem(me + i, 16)
            pltpu.make_async_remote_copy(
                src_ref=sbuf.at[s, :, q],
                dst_ref=rbuf.at[s, :, me],
                send_sem=zs.at[s],
                recv_sem=zr.at[s],
                device_id=zc_peer(q),
                device_id_type=MESH,
            ).start()
            return 0

        lax.fori_loop(1, 16, step, 0)

    def z_arrived(s):
        pltpu.make_async_copy(rbuf.at[s], rbuf.at[s], zr.at[s]).wait()

    def sends_done(s, _):
        y_copy(s).wait_send()
        pltpu.make_async_copy(sbuf.at[s, :, pl.ds(0, 15)], sbuf.at[s, :, pl.ds(0, 15)], zs.at[s]).wait()
        return 0

    def gates(k):
        lanes = pl.ds(pl.multiple_of(k * CH, CH), CH)
        return gi_ref[:, lanes], go_ref[:, lanes]

    def make_dmon(k, h, mine):
        _, go = gates(k)

        def step(j, _):
            row = pl.ds(pl.multiple_of(j * 64 + h * 32, 32), 32)
            xw = xv[k, row, :].astype(F32)
            cw = cv[k, row, :].astype(F32)
            sig = jax.nn.sigmoid(xw * go)
            dm = cw * sig
            p1[k, row, :] = dm * (1.0 - sig)
            piece = dm.astype(BF16).reshape(2, 16, CH)
            if mine:
                sbuf[DMON * K + k, h, pl.ds(j * 2, 2)] = piece
            else:
                tbuf[DMON * K + k, pl.ds(j * 2, 2)] = piece
            return 0

        lax.fori_loop(0, 8, step, 0)

    def make_halves(s, left, right):
        tbuf[s] = dot(left[oth], right).astype(BF16).reshape(16, 16, CH)
        sbuf[s, yh] = dot(left[yh], right).astype(BF16).reshape(16, 16, CH)

    def make_hidden(k):
        gi, _ = gates(k)

        def step(j, _):
            row = pl.ds(pl.multiple_of(j * 32, 32), 32)
            hv[k, row, :] = (xv[k, row, :].astype(F32) * gi).astype(BF16)
            return 0

        lax.fori_loop(0, 16, step, 0)

    def make_mix(k):
        make_hidden(k)
        make_halves(MIX * K + k, rr2, hv[k])

    rr2 = rr.reshape(2, 256, N)

    def flat(s):
        return rbuf[s].reshape(N, CH)

    def on_dmon(k):
        make_halves(DMIX * K + k, wt, flat(DMON * K + k))

    def on_mix(k):
        m = flat(MIX * K + k)
        make_halves(MON * K + k, ww, m)
        lacc[...] += dot_nt(m, flat(DMON * K + k))

    def fold(v):
        return v.reshape(4, 8, CH).sum(axis=0)

    def on_dmix(k):
        dm = flat(DMIX * K + k)
        dh[k] = dot(rt[...], dm)
        racc[...] += dot_nt(dm, hv[k])

        def step(j, acc):
            row = pl.ds(pl.multiple_of(j * 32, 32), 32)
            return acc + fold(dh[k, row, :] * xv[k, row, :].astype(F32))

        acc = lax.fori_loop(0, 16, step, jnp.zeros((8, CH), F32))
        gacc[k, 0:1, :] = acc.sum(axis=0, keepdims=True)

    def store_out(k):
        return pltpu.make_async_copy(out.at[k], o_hbm.at[0, :, pl.ds(k * CH, CH)], out_sem.at[k])

    def on_mon(k):
        gi, go = gates(k)

        def step(j, acc):
            h, w = j // 8, j % 8
            row = pl.ds(pl.multiple_of(w * 64 + h * 32, 32), 32)
            mon = rbuf[MON * K + k, h, pl.ds(w * 2, 2)].reshape(32, CH).astype(F32)
            dpre = p1[k, row, :] * mon
            gg = (dpre * go).astype(BF16).astype(F32)
            out[k, row, :] = (gg + dh[k, row, :] * gi).astype(BF16)
            return acc + fold(dpre * xv[k, row, :].astype(F32))

        acc = lax.fori_loop(0, 16, step, jnp.zeros((8, CH), F32))
        gacc[k, 1:2, :] = acc.sum(axis=0, keepdims=True)

    def spread(buf, i_sem, peer_of, mine, n):
        def step(i, _):
            pltpu.make_async_remote_copy(
                src_ref=buf.at[mine],
                dst_ref=buf.at[mine],
                send_sem=sm_s.at[i_sem],
                recv_sem=sm_r.at[i_sem],
                device_id=peer_of(lax.rem(mine + i, n)),
                device_id_type=MESH,
            ).start()
            return 0

        lax.fori_loop(1, n, step, 0)

    def spread_wait(buf, i_sem, n):
        part = buf.at[pl.ds(0, n - 1)]
        pltpu.make_async_copy(part, part, sm_r.at[i_sem]).wait()
        pltpu.make_async_copy(part, part, sm_s.at[i_sem]).wait()

    def scatter(src, dst, i_sem, peer_of, mine):
        def step(i, _):
            q = lax.rem(mine + i, 4)
            pltpu.make_async_remote_copy(
                src_ref=src.at[q],
                dst_ref=dst.at[mine],
                send_sem=rs_s.at[i_sem],
                recv_sem=rs_r.at[i_sem],
                device_id=peer_of(q),
                device_id_type=MESH,
            ).start()
            return 0

        lax.fori_loop(1, 4, step, 0)

    def scatter_wait(src, dst, i_sem):
        got, sent = dst.at[pl.ds(0, 3)], src.at[pl.ds(0, 3)]
        pltpu.make_async_copy(got, got, rs_r.at[i_sem]).wait()
        pltpu.make_async_copy(sent, sent, rs_s.at[i_sem]).wait()

    def yl_peer(q):
        return (xx * 4 + q, seq)

    def build_left():
        r, c = iota((N, N), 0), iota((N, N), 1)
        perm = ((r % 16 == c // 32) & (natural(r // 16) == c % 32)).astype(F32).astype(BF16)
        rows = dot(perm, l_ref[...].reshape(N, 32)).astype(BF16)
        e = iota((32, N), 0) == natural(iota((32, N), 1) // 16)
        wide = dot(rows, e.astype(F32).astype(BF16))
        w = jnp.where(r % 16 == c % 16, wide, 0.0).astype(BF16)
        eye = (r == c).astype(F32).astype(BF16)
        ww[...] = w.reshape(2, 256, N)
        wt[...] = dot_nt(eye, w).astype(BF16).reshape(2, 256, N)
        rt[...] = dot_nt(eye, rr[...].reshape(N, N)).astype(BF16)

    def split(v):
        hi = v.astype(BF16)
        rest = v - hi.astype(F32)
        mid = rest.astype(BF16)
        return hi, mid, (rest - mid.astype(F32)).astype(BF16)

    def left_grad():
        r, c = iota((N, N), 0), iota((N, N), 1)
        kept = jnp.where(r % 16 == c % 16, lacc[...], 0.0)
        e = (iota((32, N), 0) == iota((32, N), 1) // 16).astype(F32).astype(BF16)
        hi, mid, low = split(kept)
        lx[xx] = dot(e, hi) + dot(e, mid) + dot(e, low)

    def left_out():
        g = (ly[0] + ly[1] + ly[2] + ly[3]) * (1.0 / 128.0)
        r, c = iota((N, N), 0), iota((N, N), 1)
        perm = ((c % 16 == r // 32) & (natural(c // 16) == r % 32)).astype(F32).astype(BF16)
        cols = (natural(iota((32, 32), 0)) == iota((32, 32), 1)).astype(F32).astype(BF16)
        total = jnp.zeros((N, 32), F32)
        for part in split(g):
            total = total + dot(dot_nt(perm, part).astype(BF16), cols)
        dl_ref[...] = total.reshape(16, 32, 32)

    def right_1():
        gxs[...] = racc[...].astype(BF16).reshape(4, 128, N)
        scatter(gxs, gxr, 0, x_peer, xx)

    def right_2():
        scatter_wait(gxs, gxr, 0)
        own = racc[pl.ds(pl.multiple_of(xx * 128, 128), 128), :]
        for i in range(1, 4):
            own = own + gxr[lax.rem(xx + i, 4)].astype(F32)
        racc[0:128, :] = own
        gys[...] = own.astype(BF16).reshape(4, 32, N)
        scatter(gys, gyr, 1, yl_peer, yl)

    def right_3():
        scatter_wait(gys, gyr, 1)
        own = racc[pl.ds(pl.multiple_of(yl * 32, 32), 32), :]
        for i in range(1, 4):
            own = own + gyr[lax.rem(yl + i, 4)].astype(F32)
        fin[xx, yl] = (own * (1.0 / 128.0)).astype(BF16)
        spread(fin.at[xx], 2, yl_peer, yl, 4)

    def right_4():
        spread_wait(fin.at[xx], 2, 4)
        spread(fin, 3, x_peer, xx, 4)

    right_store = pltpu.make_async_copy(drv, dr_hbm, out_sem.at[K])

    def right_5():
        spread_wait(fin, 3, 4)

        def step(j, _):
            drv[j % 8, j // 8] = fin[j // 4, j % 4].astype(F32)
            return 0

        lax.fori_loop(0, 16, step, 0)
        right_store.start()

    lacc[...] = jnp.zeros_like(lacc)
    racc[...] = jnp.zeros_like(racc)
    for k in range(K):
        load_x(k).wait()
        load_c(k).wait()
        make_dmon(k, oth, False)
        if k == 0:
            pl.semaphore_wait(barrier, 25)
        if k < 2:
            y_copy(k).start()
        make_dmon(k, yh, True)
    for h in range(2):
        load_r(h).wait()
    make_mix(0)
    build_left()

    last = 4 * K

    def slot(t):
        y_arrived(t)

        @pl.when(t + 2 < last)
        def _():
            y_copy(t + 2).start()

        z_send(t)

    slot(0)

    def phase_dmon(k, _):
        make_mix(k)
        slot(DMON * K + k)
        z_arrived(DMON * K + k - 1)
        on_dmon(k - 1)
        return 0

    lax.fori_loop(1, K, phase_dmon, 0)
    slot(MIX * K)
    z_arrived(MIX * K - 1)
    on_dmon(K - 1)

    def phase_mix(k, _):
        slot(MIX * K + k)
        z_arrived(MIX * K + k - 1)
        on_mix(k - 1)
        return 0

    lax.fori_loop(1, K, phase_mix, 0)
    slot(DMIX * K)
    z_arrived(DMIX * K - 1)
    on_mix(K - 1)
    left_grad()
    spread(lx, 0, x_peer, xx, 4)

    def phase_dmix(k, _):
        slot(DMIX * K + k)
        z_arrived(DMIX * K + k - 1)
        on_dmix(k - 1)
        return 0

    lax.fori_loop(1, K, phase_dmix, 0)
    spread_wait(lx, 0, 4)
    ly[yl] = lx[0] + lx[1] + lx[2] + lx[3]
    spread(ly, 1, yl_peer, yl, 4)

    slot(MON * K)
    z_arrived(MON * K - 1)
    on_dmix(K - 1)
    right_1()
    for k in range(1, K):
        slot(MON * K + k)
        z_arrived(MON * K + k - 1)
        on_mon(k - 1)
        store_out(k - 1).start()
        if k == 1:
            right_2()
            spread_wait(ly, 1, 4)
            left_out()
        if k == 2:
            right_3()
        if k == 3:
            right_4()
    z_arrived(last - 1)
    on_mon(K - 1)
    store_out(K - 1).start()
    ga[me] = jnp.concatenate([gacc[k] for k in range(K)], axis=1)
    spread(ga, 4, zc_peer, me, 16)
    right_5()
    spread_wait(ga, 4, 16)
    gb[xx] = ga[...].sum(axis=0)
    spread(gb, 5, x_peer, xx, 4)
    spread_wait(gb, 5, 4)
    gc[ring] = gb[...].sum(axis=0)
    spread(gc, 6, y_peer, ring, 8)
    spread_wait(gc, 6, 8)
    total = gc[...].sum(axis=0) * (1.0 / 512.0)
    dgi_ref[...] = total[0:1]
    dgo_ref[...] = total[1:2]
    lax.fori_loop(0, last, sends_done, 0)
    for k in range(K):
        store_out(k).wait()
    right_store.wait()


def on_device(inputs, cotangent, block_right, block_left, gate_in, gate_out):
    hbm = pl.BlockSpec(memory_space=pl.ANY)
    vmem = pl.BlockSpec(memory_space=pltpu.VMEM)
    sub = 4 * K
    scratch = [
        pltpu.VMEM((K, N, CH), BF16),
        pltpu.VMEM((K, N, CH), BF16),
        pltpu.VMEM((K, N, CH), BF16),
        pltpu.VMEM((K, N, CH), F32),
        pltpu.VMEM((K, N, CH), F32),
        pltpu.VMEM((K, N, CH), BF16),
        pltpu.VMEM((2, 8, 32, N), BF16),
        pltpu.VMEM((N, N), BF16),
        pltpu.VMEM((2, 256, N), BF16),
        pltpu.VMEM((2, 256, N), BF16),
        pltpu.VMEM((sub, 16, 16, CH), BF16),
        pltpu.VMEM((sub, 2, 16, 16, CH), BF16),
        pltpu.VMEM((sub, 2, 16, 16, CH), BF16),
        pltpu.VMEM((N, N), F32),
        pltpu.VMEM((N, N), F32),
        pltpu.VMEM((K, 2, CH), F32),
        pltpu.VMEM((4, 128, N), BF16),
        pltpu.VMEM((4, 128, N), BF16),
        pltpu.VMEM((4, 32, N), BF16),
        pltpu.VMEM((4, 32, N), BF16),
        pltpu.VMEM((4, 4, 32, N), BF16),
        pltpu.VMEM((8, 2, 32, N), F32),
        pltpu.VMEM((4, 32, N), F32),
        pltpu.VMEM((4, 32, N), F32),
        pltpu.VMEM((16, 2, D), F32),
        pltpu.VMEM((4, 2, D), F32),
        pltpu.VMEM((8, 2, D), F32),
        pltpu.SemaphoreType.DMA((2 * K + 2,)),
        pltpu.SemaphoreType.DMA((K + 1,)),
        pltpu.SemaphoreType.DMA((sub,)),
        pltpu.SemaphoreType.DMA((sub,)),
        pltpu.SemaphoreType.DMA((sub,)),
        pltpu.SemaphoreType.DMA((sub,)),
        pltpu.SemaphoreType.DMA((2,)),
        pltpu.SemaphoreType.DMA((2,)),
        pltpu.SemaphoreType.DMA((7,)),
        pltpu.SemaphoreType.DMA((7,)),
    ]
    d_inputs, d_right, d_left, d_gin, d_gout = pl.pallas_call(
        kernel,
        out_shape=(
            jax.ShapeDtypeStruct((1, N, D), BF16),
            jax.ShapeDtypeStruct((8, 2, 32, N), F32),
            jax.ShapeDtypeStruct((16, 32, 32), F32),
            jax.ShapeDtypeStruct((1, D), F32),
            jax.ShapeDtypeStruct((1, D), F32),
        ),
        in_specs=[hbm, hbm, hbm, vmem, vmem, vmem],
        out_specs=(hbm, hbm, vmem, vmem, vmem),
        scratch_shapes=scratch,
        compiler_params=pltpu.CompilerParams(
            collective_id=0, has_side_effects=True, vmem_limit_bytes=50 * 1024 * 1024
        ),
        name="monarch",
    )(
        inputs,
        cotangent,
        block_right.reshape(8, 2, 32, N),
        block_left,
        gate_in.reshape(1, D),
        gate_out.reshape(1, D),
    )
    return (
        d_inputs,
        d_right.reshape(1, N, N),
        d_left,
        d_gin.reshape(D),
        d_gout.reshape(D),
    )


def solution(mesh):
    in_specs = (
        P("dp", "seq", None),
        P("dp", "seq", None),
        P("seq", None, None),
        P("seq", None, None),
        P(),
        P(),
    )
    out_specs = (P("dp", "seq", None), P("seq", None, None), P("seq", None, None), P(), P())
    return jax.shard_map(
        on_device, mesh=mesh, in_specs=in_specs, out_specs=out_specs, check_vma=False
    )
```

```python
import functools

import jax
import jax.numpy as jnp
from jax import lax
from jax.experimental import pallas as pl
from jax.experimental.pallas import tpu as pltpu
from jax.sharding import PartitionSpec as P

MESH = pl.DeviceIdType.MESH
F32 = jnp.float32
BF16 = jnp.bfloat16
K = 4
D = 1024
CH = D // K
N = 512
DMON, DMIX, MIX, MON = 0, 1, 2, 3
NT = (((1,), (1,)), ((), ()))


def dot(a, b):
    return jnp.dot(a, b, preferred_element_type=F32)


def dot_nt(a, b):
    return lax.dot_general(a, b, NT, preferred_element_type=F32)


def natural(p):
    return ((p // 2) % 8) * 4 + (p // 16) * 2 + p % 2


def iota(shape, dim):
    return lax.broadcasted_iota(jnp.int32, shape, dim)


def kernel(
    x_hbm, c_hbm, r_hbm, l_hbm, gi_hbm, go_hbm,
    o_ref, dr_ref, dl_ref, dgi_ref, dgo_ref,
    l_ref, gi_ref, go_ref, xv, cv, hv, p1, dh, rr, rt, ww, wt,
    tbuf, sbuf, rbuf, racc, lacc,
    gxs, gxr, gys, gyr, fin, lx, lxr, ly, lf, ga, gb, gc,
    in_sem, ys, yr, zs, zr, rs_s, rs_r, sm_s, sm_r,
):
    dp = lax.axis_index("dp")
    seq = lax.axis_index("seq")
    xx, yl = dp // 4, dp % 4
    z, yh, core = seq // 4, (seq // 2) % 2, seq % 2
    oth = 1 - yh
    me = z * 2 + core
    ring = yh * 4 + yl

    def zc_peer(q):
        return (dp, (q // 2) * 4 + yh * 2 + q % 2)

    def x_peer(q):
        return (q * 4 + yl, seq)

    def y_peer(q):
        return (xx * 4 + q % 4, z * 4 + (q // 4) * 2 + core)

    partner = (dp, z * 4 + oth * 2 + core)

    def load_x(k):
        return pltpu.make_async_copy(x_hbm.at[0, :, pl.ds(k * CH, CH)], xv.at[k], in_sem.at[k])

    def load_c(k):
        return pltpu.make_async_copy(c_hbm.at[0, :, pl.ds(k * CH, CH)], cv.at[k], in_sem.at[K + k])

    def load_r(h):
        return pltpu.make_async_copy(r_hbm.at[:, h], rr.at[h], in_sem.at[2 * K + h])

    def load_small():
        pairs = ((l_hbm, l_ref), (gi_hbm, gi_ref), (go_hbm, go_ref))
        return [
            pltpu.make_async_copy(a, b, in_sem.at[2 * K + 2 + i]) for i, (a, b) in enumerate(pairs)
        ]

    load_x(0).start()
    load_c(0).start()
    for copy in load_small():
        copy.start()
    for k in range(1, K):
        load_x(k).start()
        load_c(k).start()
    for h in range(2):
        load_r(h).start()

    barrier = pltpu.get_barrier_semaphore()

    def greet(peer_of, mine, n):
        def step(i, _):
            pl.semaphore_signal(
                barrier, inc=1, device_id=peer_of(lax.rem(mine + i, n)), device_id_type=MESH
            )
            return 0

        lax.fori_loop(1, n, step, 0)

    greet(zc_peer, me, 16)
    greet(x_peer, xx, 4)
    greet(y_peer, ring, 8)

    def y_copy(s):
        return pltpu.make_async_remote_copy(
            src_ref=tbuf.at[s],
            dst_ref=sbuf.at[s, yh],
            send_sem=ys.at[s],
            recv_sem=yr.at[s],
            device_id=partner,
            device_id_type=MESH,
        )

    def y_arrived(s):
        pltpu.make_async_copy(sbuf.at[s, oth], sbuf.at[s, oth], yr.at[s]).wait()

    def z_send(s, h):
        pltpu.make_async_copy(sbuf.at[s, h, me], rbuf.at[s, h, me], zr.at[s]).start()

        def step(i, _):
            q = lax.rem(me + i, 16)
            pltpu.make_async_remote_copy(
                src_ref=sbuf.at[s, h, q],
                dst_ref=rbuf.at[s, h, me],
                send_sem=zs.at[s],
                recv_sem=zr.at[s],
                device_id=zc_peer(q),
                device_id_type=MESH,
            ).start()
            return 0

        lax.fori_loop(1, 16, step, 0)

    def z_arrived(s):
        pltpu.make_async_copy(rbuf.at[s], rbuf.at[s], zr.at[s]).wait()

    def sends_done(s, _):
        y_copy(s).wait_send()
        pltpu.make_async_copy(sbuf.at[s, :, pl.ds(0, 15)], sbuf.at[s, :, pl.ds(0, 15)], zs.at[s]).wait()
        return 0

    def gates(k):
        lanes = pl.ds(pl.multiple_of(k * CH, CH), CH)
        return gi_ref[:, lanes], go_ref[:, lanes]

    def make_dmon(k, h, mine):
        _, go = gates(k)

        def step(j, _):
            row = pl.ds(pl.multiple_of(j * 64 + h * 32, 32), 32)
            xw = xv[k, row, :].astype(F32)
            cw = cv[k, row, :].astype(F32)
            sig = jax.nn.sigmoid(xw * go)
            dm = cw * sig
            p1[k, row, :] = dm * (1.0 - sig)
            piece = dm.astype(BF16).reshape(2, 16, CH)
            if mine:
                sbuf[DMON * K + k, h, pl.ds(j * 2, 2)] = piece
            else:
                tbuf[DMON * K + k, pl.ds(j * 2, 2)] = piece
            return 0

        lax.fori_loop(0, 8, step, 0)

    def make_halves(s, left, right):
        tbuf[s] = dot(left[oth], right).astype(BF16).reshape(16, 16, CH)
        sbuf[s, yh] = dot(left[yh], right).astype(BF16).reshape(16, 16, CH)

    def make_hidden(k):
        gi, _ = gates(k)

        def step(j, _):
            row = pl.ds(pl.multiple_of(j * 32, 32), 32)
            hv[k, row, :] = (xv[k, row, :].astype(F32) * gi).astype(BF16)
            return 0

        lax.fori_loop(0, 16, step, 0)

    def make_mix(k):
        make_hidden(k)
        make_halves(MIX * K + k, rr2, hv[k])

    rr2 = rr.reshape(2, 256, N)

    def flat(s):
        return rbuf[s].reshape(N, CH)

    def launch(s):
        y_copy(s).start()
        z_send(s, yh)

    def on_dmon(k):
        make_halves(DMIX * K + k, wt, flat(DMON * K + k))
        launch(DMIX * K + k)

    def on_mix(k):
        m = flat(MIX * K + k)
        make_halves(MON * K + k, ww, m)
        launch(MON * K + k)
        lacc[...] += dot_nt(m, flat(DMON * K + k))

    def fold(v):
        return v.reshape(4, 8, CH).sum(axis=0)

    def on_dmix(k):
        dm = flat(DMIX * K + k)
        dh[k] = dot(rt[...], dm)
        racc[...] += dot_nt(dm, hv[k])

        def step(j, acc):
            row = pl.ds(pl.multiple_of(j * 32, 32), 32)
            return acc + fold(dh[k, row, :] * xv[k, row, :].astype(F32))

        acc = lax.fori_loop(0, 16, step, jnp.zeros((8, CH), F32))
        ga[0, me, k] = acc.sum(axis=0, keepdims=True)

    def on_mon(k):
        gi, go = gates(k)

        def step(j, acc):
            h, w = j // 8, j % 8
            row = pl.ds(pl.multiple_of(w * 64 + h * 32, 32), 32)
            mon = rbuf[MON * K + k, h, pl.ds(w * 2, 2)].reshape(32, CH).astype(F32)
            dpre = p1[k, row, :] * mon
            gg = (dpre * go).astype(BF16).astype(F32)
            o_ref[0, row, k * CH : (k + 1) * CH] = (gg + dh[k, row, :] * gi).astype(BF16)
            return acc + fold(dpre * xv[k, row, :].astype(F32))

        acc = lax.fori_loop(0, 16, step, jnp.zeros((8, CH), F32))
        ga[1, me, k] = acc.sum(axis=0, keepdims=True)

    def spread(buf, i_sem, peer_of, mine, n):
        def step(i, _):
            pltpu.make_async_remote_copy(
                src_ref=buf.at[mine],
                dst_ref=buf.at[mine],
                send_sem=sm_s.at[i_sem],
                recv_sem=sm_r.at[i_sem],
                device_id=peer_of(lax.rem(mine + i, n)),
                device_id_type=MESH,
            ).start()
            return 0

        lax.fori_loop(1, n, step, 0)

    def spread_wait(buf, i_sem, n):
        part = buf.at[pl.ds(0, n - 1)]
        pltpu.make_async_copy(part, part, sm_r.at[i_sem]).wait()
        pltpu.make_async_copy(part, part, sm_s.at[i_sem]).wait()

    def scatter(src, dst, i_sem, peer_of, mine):
        def step(i, _):
            q = lax.rem(mine + i, 4)
            pltpu.make_async_remote_copy(
                src_ref=src.at[q],
                dst_ref=dst.at[mine],
                send_sem=rs_s.at[i_sem],
                recv_sem=rs_r.at[i_sem],
                device_id=peer_of(q),
                device_id_type=MESH,
            ).start()
            return 0

        lax.fori_loop(1, 4, step, 0)

    def scatter_wait(src, dst, i_sem):
        got, sent = dst.at[pl.ds(0, 3)], src.at[pl.ds(0, 3)]
        pltpu.make_async_copy(got, got, rs_r.at[i_sem]).wait()
        pltpu.make_async_copy(sent, sent, rs_s.at[i_sem]).wait()

    def yl_peer(q):
        return (xx * 4 + q, seq)

    def build_left():
        r, c = iota((N, N), 0), iota((N, N), 1)
        perm = ((r % 16 == c // 32) & (natural(r // 16) == c % 32)).astype(F32).astype(BF16)
        rows = dot(perm, l_ref[...].reshape(N, 32)).astype(BF16)
        e = iota((32, N), 0) == natural(iota((32, N), 1) // 16)
        wide = dot(rows, e.astype(F32).astype(BF16))
        w = jnp.where(r % 16 == c % 16, wide, 0.0).astype(BF16)
        eye = (r == c).astype(F32).astype(BF16)
        ww[...] = w.reshape(2, 256, N)
        wt[...] = dot_nt(eye, w).astype(BF16).reshape(2, 256, N)
        rt[...] = dot_nt(eye, rr[...].reshape(N, N)).astype(BF16)

    def split(v):
        hi = v.astype(BF16)
        rest = v - hi.astype(F32)
        mid = rest.astype(BF16)
        return hi, mid, (rest - mid.astype(F32)).astype(BF16)

    def left_1():
        r, c = iota((N, N), 0), iota((N, N), 1)
        kept = jnp.where(r % 16 == c % 16, lacc[...], 0.0)
        e = (iota((32, N), 0) == iota((32, N), 1) // 16).astype(F32).astype(BF16)
        hi, mid, low = split(kept)
        lx[...] = (dot(e, hi) + dot(e, mid) + dot(e, low)).reshape(4, 8, N)
        scatter(lx, lxr, 2, x_peer, xx)

    def left_2():
        scatter_wait(lx, lxr, 2)
        own = lx[xx]
        for i in range(1, 4):
            own = own + lxr[lax.rem(xx + i, 4)]
        ly[yl] = own
        spread(ly, 0, yl_peer, yl, 4)

    def left_3():
        spread_wait(ly, 0, 4)
        lf[xx] = (ly[0] + ly[1] + ly[2] + ly[3]) * (1.0 / 128.0)
        spread(lf, 1, x_peer, xx, 4)

    def left_out():
        spread_wait(lf, 1, 4)
        g = lf[...].reshape(32, N)
        r, c = iota((N, N), 0), iota((N, N), 1)
        perm = ((c % 16 == r // 32) & (natural(c // 16) == r % 32)).astype(F32).astype(BF16)
        cols = (natural(iota((32, 32), 0)) == iota((32, 32), 1)).astype(F32).astype(BF16)
        total = jnp.zeros((N, 32), F32)
        for part in split(g):
            total = total + dot(dot_nt(perm, part).astype(BF16), cols)
        dl_ref[...] = total.reshape(16, 32, 32)

    def right_1():
        gxs[...] = racc[...].astype(BF16).reshape(4, 128, N)
        scatter(gxs, gxr, 0, x_peer, xx)

    def right_2():
        scatter_wait(gxs, gxr, 0)
        own = racc[pl.ds(pl.multiple_of(xx * 128, 128), 128), :]
        for i in range(1, 4):
            own = own + gxr[lax.rem(xx + i, 4)].astype(F32)
        racc[0:128, :] = own
        gys[...] = own.astype(BF16).reshape(4, 32, N)
        scatter(gys, gyr, 1, yl_peer, yl)

    def right_3():
        scatter_wait(gys, gyr, 1)
        own = racc[pl.ds(pl.multiple_of(yl * 32, 32), 32), :]
        for i in range(1, 4):
            own = own + gyr[lax.rem(yl + i, 4)].astype(F32)
        fin[xx, yl] = (own * (1.0 / 128.0)).astype(BF16)
        spread(fin.at[xx], 2, yl_peer, yl, 4)

    def right_4():
        spread_wait(fin.at[xx], 2, 4)
        spread(fin, 3, x_peer, xx, 4)

    def right_5():
        spread_wait(fin, 3, 4)

        def step(j, _):
            dr_ref[j % 8, j // 8] = fin[j // 4, j % 4].astype(F32)
            return 0

        lax.fori_loop(0, 16, step, 0)

    def gate_1(g):
        spread(ga.at[g], 4 + g, zc_peer, me, 16)

    def gate_2(g):
        spread_wait(ga.at[g], 4 + g, 16)
        gb[g, xx] = ga[g].sum(axis=0)
        spread(gb.at[g], 6 + g, x_peer, xx, 4)

    def gate_3(g):
        spread_wait(gb.at[g], 6 + g, 4)
        gc[g, ring] = gb[g].sum(axis=0)
        spread(gc.at[g], 8 + g, y_peer, ring, 8)

    def gate_4(g, out_ref):
        spread_wait(gc.at[g], 8 + g, 8)
        total = gc[g].sum(axis=0) * (1.0 / 512.0)
        for k in range(K):
            out_ref[:, k * CH : (k + 1) * CH] = total[k]

    lacc[...] = jnp.zeros_like(lacc)
    racc[...] = jnp.zeros_like(racc)
    for copy in load_small():
        copy.wait()
    for k in range(K):
        load_x(k).wait()
        load_c(k).wait()
        make_dmon(k, oth, False)
        make_dmon(k, yh, True)
    pl.semaphore_wait(barrier, 25)
    y_copy(0).start()
    z_send(0, yh)
    z_send(1, yh)
    y_copy(1).start()
    z_send(2, yh)
    z_send(3, yh)
    for h in range(2):
        load_r(h).wait()
    build_left()
    for k in range(K):
        make_mix(k)

    last = 4 * K

    def slot(t):
        y_arrived(t)
        z_send(t, oth)

    def after(t, on, k):
        z_arrived(t)
        on(k)

    slot(0)
    y_copy(2).start()
    z_send(8, yh)
    slot(1)
    y_copy(3).start()
    z_send(9, yh)
    after(0, on_dmon, 0)
    slot(2)
    z_send(10, yh)
    after(1, on_dmon, 1)
    slot(3)
    z_send(11, yh)
    after(2, on_dmon, 2)
    slot(4)
    after(3, on_dmon, 3)

    def middle(k, _):
        slot(DMIX * K + k)
        y_copy(MIX * K + k - 1).start()
        after(DMIX * K + k - 1, on_dmix, k - 1)
        return 0

    lax.fori_loop(1, K, middle, 0)
    slot(8)
    y_copy(11).start()
    after(7, on_dmix, 3)
    right_1()
    gate_1(0)
    slot(9)
    after(8, on_mix, 0)
    slot(10)
    after(9, on_mix, 1)
    slot(11)
    after(10, on_mix, 2)
    right_2()
    gate_2(0)
    slot(12)
    after(11, on_mix, 3)
    left_1()
    slot(13)
    gate_3(0)
    after(12, on_mon, 0)
    slot(14)
    after(13, on_mon, 1)
    right_3()
    left_2()
    slot(15)
    after(14, on_mon, 2)
    right_4()
    left_3()
    gate_4(0, dgi_ref)
    after(15, on_mon, 3)
    gate_1(1)
    gate_2(1)
    right_5()
    gate_3(1)
    left_out()
    lax.fori_loop(0, last, sends_done, 0)
    gate_4(1, dgo_ref)


def copy_kernel(*refs):
    n = len(refs) // 2
    sem = refs[-1]
    copies = [pltpu.make_async_copy(refs[i], refs[n + i], sem.at[i]) for i in range(n)]
    for copy in copies:
        copy.start()
    for copy in copies:
        copy.wait()


def on_device(inputs, cotangent, block_right, block_left, gate_in, gate_out):
    hbm = pl.BlockSpec(memory_space=pltpu.HBM)
    vmem = pl.BlockSpec(memory_space=pltpu.VMEM)
    sub = 4 * K
    scratch = [
        pltpu.VMEM((16, 32, 32), BF16),
        pltpu.VMEM((1, D), F32),
        pltpu.VMEM((1, D), F32),
        pltpu.VMEM((K, N, CH), BF16),
        pltpu.VMEM((K, N, CH), BF16),
        pltpu.VMEM((K, N, CH), BF16),
        pltpu.VMEM((K, N, CH), F32),
        pltpu.VMEM((K, N, CH), F32),
        pltpu.VMEM((2, 8, 32, N), BF16),
        pltpu.VMEM((N, N), BF16),
        pltpu.VMEM((2, 256, N), BF16),
        pltpu.VMEM((2, 256, N), BF16),
        pltpu.VMEM((sub, 16, 16, CH), BF16),
        pltpu.VMEM((sub, 2, 16, 16, CH), BF16),
        pltpu.VMEM((sub, 2, 16, 16, CH), BF16),
        pltpu.VMEM((N, N), F32),
        pltpu.VMEM((N, N), F32),
        pltpu.VMEM((4, 128, N), BF16),
        pltpu.VMEM((4, 128, N), BF16),
        pltpu.VMEM((4, 32, N), BF16),
        pltpu.VMEM((4, 32, N), BF16),
        pltpu.VMEM((4, 4, 32, N), BF16),
        pltpu.VMEM((4, 8, N), F32),
        pltpu.VMEM((4, 8, N), F32),
        pltpu.VMEM((4, 8, N), F32),
        pltpu.VMEM((4, 8, N), F32),
        pltpu.VMEM((2, 16, K, 1, CH), F32),
        pltpu.VMEM((2, 4, K, 1, CH), F32),
        pltpu.VMEM((2, 8, K, 1, CH), F32),
        pltpu.SemaphoreType.DMA((2 * K + 5,)),
        pltpu.SemaphoreType.DMA((sub,)),
        pltpu.SemaphoreType.DMA((sub,)),
        pltpu.SemaphoreType.DMA((sub,)),
        pltpu.SemaphoreType.DMA((sub,)),
        pltpu.SemaphoreType.DMA((3,)),
        pltpu.SemaphoreType.DMA((3,)),
        pltpu.SemaphoreType.DMA((10,)),
        pltpu.SemaphoreType.DMA((10,)),
    ]
    shapes = (
        ((1, N, D), BF16),
        ((8, 2, 32, N), F32),
        ((16, 32, 32), F32),
        ((1, D), F32),
        ((1, D), F32),
    )
    results = pl.pallas_call(
        kernel,
        out_shape=tuple(pltpu.VMEM(*shape) for shape in shapes),
        in_specs=[hbm] * 6,
        out_specs=(vmem,) * 5,
        scratch_shapes=scratch,
        compiler_params=pltpu.CompilerParams(
            collective_id=0, has_side_effects=True, vmem_limit_bytes=50 * 1024 * 1024
        ),
        name="monarch",
    )(
        *(
            pltpu.with_memory_space_constraint(a, pltpu.HBM)
            for a in (
                inputs,
                cotangent,
                block_right.reshape(8, 2, 32, N),
                block_left,
                gate_in.reshape(1, D),
                gate_out.reshape(1, D),
            )
        )
    )
    d_inputs, d_right, d_left, d_gin, d_gout = pl.pallas_call(
        copy_kernel,
        out_shape=tuple(jax.ShapeDtypeStruct(*shape) for shape in shapes),
        in_specs=[vmem] * 5,
        out_specs=(hbm,) * 5,
        scratch_shapes=[pltpu.SemaphoreType.DMA((5,))],
        name="results",
    )(*(pltpu.with_memory_space_constraint(r, pltpu.VMEM) for r in results))
    return (
        d_inputs,
        d_right.reshape(1, N, N),
        d_left,
        d_gin.reshape(D),
        d_gout.reshape(D),
    )


def solution(mesh):
    in_specs = (
        P("dp", "seq", None),
        P("dp", "seq", None),
        P("seq", None, None),
        P("seq", None, None),
        P(),
        P(),
    )
    out_specs = (P("dp", "seq", None), P("seq", None, None), P("seq", None, None), P(), P())
    return jax.shard_map(
        on_device, mesh=mesh, in_specs=in_specs, out_specs=out_specs, check_vma=False
    )
```

```python
import functools

import jax
import jax.numpy as jnp
from jax import lax
from jax.experimental import pallas as pl
from jax.experimental.pallas import tpu as pltpu
from jax.sharding import PartitionSpec as P

MESH = pl.DeviceIdType.MESH
F32 = jnp.float32
BF16 = jnp.bfloat16
K = 8
D = 1024
CH = D // K
N = 512
DMON, DMIX, MIX, MON = 0, 1, 2, 3
NT = (((1,), (1,)), ((), ()))


def dot(a, b):
    return jnp.dot(a, b, preferred_element_type=F32)


def dot_nt(a, b):
    return lax.dot_general(a, b, NT, preferred_element_type=F32)


def natural(p):
    return ((p // 2) % 8) * 4 + (p // 16) * 2 + p % 2


def iota(shape, dim):
    return lax.broadcasted_iota(jnp.int32, shape, dim)


def kernel(
    x_hbm, c_hbm, r_hbm, l_hbm, gi_hbm, go_hbm,
    o_ref, dr_ref, dl_ref, dgi_ref, dgo_ref,
    l_ref, gi_ref, go_ref, xv, cv, hv, p1, dh, rr, rt, ww, wt,
    tbuf, sbuf, rbuf, racc, lacc,
    gxs, gxr, gys, gyr, fin, lx, lxr, ly, lf, ga, gb, gc,
    in_sem, ys, yr, zs, zr, rs_s, rs_r, sm_s, sm_r,
):
    dp = lax.axis_index("dp")
    seq = lax.axis_index("seq")
    xx, yl = dp // 4, dp % 4
    z, yh, core = seq // 4, (seq // 2) % 2, seq % 2
    oth = 1 - yh
    me = z * 2 + core
    ring = yh * 4 + yl

    def zc_peer(q):
        return (dp, (q // 2) * 4 + yh * 2 + q % 2)

    def x_peer(q):
        return (q * 4 + yl, seq)

    def y_peer(q):
        return (xx * 4 + q % 4, z * 4 + (q // 4) * 2 + core)

    partner = (dp, z * 4 + oth * 2 + core)

    def load_x(k):
        return pltpu.make_async_copy(x_hbm.at[0, :, pl.ds(k * CH, CH)], xv.at[k], in_sem.at[k])

    def load_c(k):
        return pltpu.make_async_copy(c_hbm.at[0, :, pl.ds(k * CH, CH)], cv.at[k], in_sem.at[K + k])

    def load_r(h):
        return pltpu.make_async_copy(r_hbm.at[:, h], rr.at[h], in_sem.at[2 * K + h])

    def load_small():
        pairs = ((l_hbm, l_ref), (gi_hbm, gi_ref), (go_hbm, go_ref))
        return [
            pltpu.make_async_copy(a, b, in_sem.at[2 * K + 2 + i]) for i, (a, b) in enumerate(pairs)
        ]

    load_x(0).start()
    load_c(0).start()
    for copy in load_small():
        copy.start()

    barrier = pltpu.get_barrier_semaphore()

    def greet(peer_of, mine, n):
        def step(i, _):
            pl.semaphore_signal(
                barrier, inc=1, device_id=peer_of(lax.rem(mine + i, n)), device_id_type=MESH
            )
            return 0

        lax.fori_loop(1, n, step, 0)

    greet(zc_peer, me, 16)
    greet(x_peer, xx, 4)
    greet(y_peer, ring, 8)
    for k in range(1, K):
        load_x(k).start()
        load_c(k).start()
    for h in range(2):
        load_r(h).start()

    def y_copy(s):
        return pltpu.make_async_remote_copy(
            src_ref=tbuf.at[s],
            dst_ref=sbuf.at[s, yh],
            send_sem=ys.at[s],
            recv_sem=yr.at[s],
            device_id=partner,
            device_id_type=MESH,
        )

    def y_arrived(s):
        pltpu.make_async_copy(sbuf.at[s, oth], sbuf.at[s, oth], yr.at[s]).wait()

    def z_send(s, h):
        pltpu.make_async_copy(sbuf.at[s, h, me], rbuf.at[s, h, me], zr.at[s]).start()

        def step(i, _):
            q = lax.rem(me + i, 16)
            pltpu.make_async_remote_copy(
                src_ref=sbuf.at[s, h, q],
                dst_ref=rbuf.at[s, h, me],
                send_sem=zs.at[s],
                recv_sem=zr.at[s],
                device_id=zc_peer(q),
                device_id_type=MESH,
            ).start()
            return 0

        lax.fori_loop(1, 16, step, 0)

    def z_arrived(s):
        pltpu.make_async_copy(rbuf.at[s], rbuf.at[s], zr.at[s]).wait()

    def sends_done(s, _):
        y_copy(s).wait_send()
        pltpu.make_async_copy(sbuf.at[s, :, pl.ds(0, 15)], sbuf.at[s, :, pl.ds(0, 15)], zs.at[s]).wait()
        return 0

    def lanes_of(k):
        return pl.ds(pl.multiple_of(k * CH, CH), CH)

    def gates(k):
        return gi_ref[:, lanes_of(k)], go_ref[:, lanes_of(k)]

    def make_dmon(k, h, mine):
        _, go = gates(k)

        def step(j, _):
            row = pl.ds(pl.multiple_of(j * 64 + h * 32, 32), 32)
            xw = xv[k, row, :].astype(F32)
            cw = cv[k, row, :].astype(F32)
            sig = jax.nn.sigmoid(xw * go)
            dm = cw * sig
            p1[k, row, :] = dm * (1.0 - sig)
            piece = dm.astype(BF16).reshape(2, 16, CH)
            if mine:
                sbuf[DMON * K + k, h, pl.ds(j * 2, 2)] = piece
            else:
                tbuf[DMON * K + k, pl.ds(j * 2, 2)] = piece
            return 0

        lax.fori_loop(0, 8, step, 0)

    def make_halves(s, left, right):
        tbuf[s] = dot(left[oth], right).astype(BF16).reshape(16, 16, CH)
        sbuf[s, yh] = dot(left[yh], right).astype(BF16).reshape(16, 16, CH)

    def make_hidden(k):
        gi, _ = gates(k)

        def step(j, _):
            row = pl.ds(pl.multiple_of(j * 32, 32), 32)
            hv[k, row, :] = (xv[k, row, :].astype(F32) * gi).astype(BF16)
            return 0

        lax.fori_loop(0, 16, step, 0)

    def make_mix(k):
        make_hidden(k)
        make_halves(MIX * K + k, rr2, hv[k])

    rr2 = rr.reshape(2, 256, N)

    def flat(s):
        return rbuf[s].reshape(N, CH)

    def launch(s):
        y_copy(s).start()
        z_send(s, yh)

    def on_dmon(k):
        make_halves(DMIX * K + k, wt, flat(DMON * K + k))
        launch(DMIX * K + k)

    def on_mix(k):
        m = flat(MIX * K + k)
        make_halves(MON * K + k, ww, m)
        launch(MON * K + k)
        lacc[...] += dot_nt(m, flat(DMON * K + k))

    def fold(v):
        return v.reshape(4, 8, CH).sum(axis=0)

    def on_dmix(k):
        dm = flat(DMIX * K + k)
        dh[k] = dot(rt[...], dm)
        racc[...] += dot_nt(dm, hv[k])

        def step(j, acc):
            row = pl.ds(pl.multiple_of(j * 32, 32), 32)
            return acc + fold(dh[k, row, :] * xv[k, row, :].astype(F32))

        acc = lax.fori_loop(0, 16, step, jnp.zeros((8, CH), F32))
        ga[0, me, k] = acc.sum(axis=0, keepdims=True)

    def on_mon(k):
        gi, go = gates(k)

        def step(j, acc):
            h, w = j // 8, j % 8
            row = pl.ds(pl.multiple_of(w * 64 + h * 32, 32), 32)
            mon = rbuf[MON * K + k, h, pl.ds(w * 2, 2)].reshape(32, CH).astype(F32)
            dpre = p1[k, row, :] * mon
            gg = (dpre * go).astype(BF16).astype(F32)
            o_ref[0, row, lanes_of(k)] = (gg + dh[k, row, :] * gi).astype(BF16)
            return acc + fold(dpre * xv[k, row, :].astype(F32))

        acc = lax.fori_loop(0, 16, step, jnp.zeros((8, CH), F32))
        ga[1, me, k] = acc.sum(axis=0, keepdims=True)

    def spread(buf, i_sem, peer_of, mine, n):
        def step(i, _):
            pltpu.make_async_remote_copy(
                src_ref=buf.at[mine],
                dst_ref=buf.at[mine],
                send_sem=sm_s.at[i_sem],
                recv_sem=sm_r.at[i_sem],
                device_id=peer_of(lax.rem(mine + i, n)),
                device_id_type=MESH,
            ).start()
            return 0

        lax.fori_loop(1, n, step, 0)

    def spread_wait(buf, i_sem, n):
        part = buf.at[pl.ds(0, n - 1)]
        pltpu.make_async_copy(part, part, sm_r.at[i_sem]).wait()
        pltpu.make_async_copy(part, part, sm_s.at[i_sem]).wait()

    def scatter(src, dst, i_sem, peer_of, mine):
        def step(i, _):
            q = lax.rem(mine + i, 4)
            pltpu.make_async_remote_copy(
                src_ref=src.at[q],
                dst_ref=dst.at[mine],
                send_sem=rs_s.at[i_sem],
                recv_sem=rs_r.at[i_sem],
                device_id=peer_of(q),
                device_id_type=MESH,
            ).start()
            return 0

        lax.fori_loop(1, 4, step, 0)

    def scatter_wait(src, dst, i_sem):
        got, sent = dst.at[pl.ds(0, 3)], src.at[pl.ds(0, 3)]
        pltpu.make_async_copy(got, got, rs_r.at[i_sem]).wait()
        pltpu.make_async_copy(sent, sent, rs_s.at[i_sem]).wait()

    def yl_peer(q):
        return (xx * 4 + q, seq)

    def build_left():
        r, c = iota((N, N), 0), iota((N, N), 1)
        perm = ((r % 16 == c // 32) & (natural(r // 16) == c % 32)).astype(F32).astype(BF16)
        rows = dot(perm, l_ref[...].reshape(N, 32)).astype(BF16)
        e = iota((32, N), 0) == natural(iota((32, N), 1) // 16)
        wide = dot(rows, e.astype(F32).astype(BF16))
        w = jnp.where(r % 16 == c % 16, wide, 0.0).astype(BF16)
        eye = (r == c).astype(F32).astype(BF16)
        ww[...] = w.reshape(2, 256, N)
        wt[...] = dot_nt(eye, w).astype(BF16).reshape(2, 256, N)
        rt[...] = dot_nt(eye, rr[...].reshape(N, N)).astype(BF16)

    def split(v):
        hi = v.astype(BF16)
        rest = v - hi.astype(F32)
        mid = rest.astype(BF16)
        return hi, mid, (rest - mid.astype(F32)).astype(BF16)

    def left_1():
        r, c = iota((N, N), 0), iota((N, N), 1)
        kept = jnp.where(r % 16 == c % 16, lacc[...], 0.0)
        e = (iota((32, N), 0) == iota((32, N), 1) // 16).astype(F32).astype(BF16)
        hi, mid, low = split(kept)
        lx[...] = (dot(e, hi) + dot(e, mid) + dot(e, low)).reshape(4, 8, N)
        scatter(lx, lxr, 2, x_peer, xx)

    def left_2():
        scatter_wait(lx, lxr, 2)
        own = lx[xx]
        for i in range(1, 4):
            own = own + lxr[lax.rem(xx + i, 4)]
        ly[yl] = own
        spread(ly, 0, yl_peer, yl, 4)

    def left_3():
        spread_wait(ly, 0, 4)
        lf[xx] = (ly[0] + ly[1] + ly[2] + ly[3]) * (1.0 / 128.0)
        spread(lf, 1, x_peer, xx, 4)

    def left_out():
        spread_wait(lf, 1, 4)
        g = lf[...].reshape(32, N)
        r, c = iota((N, N), 0), iota((N, N), 1)
        perm = ((c % 16 == r // 32) & (natural(c // 16) == r % 32)).astype(F32).astype(BF16)
        cols = (natural(iota((32, 32), 0)) == iota((32, 32), 1)).astype(F32).astype(BF16)
        total = jnp.zeros((N, 32), F32)
        for part in split(g):
            total = total + dot(dot_nt(perm, part).astype(BF16), cols)
        dl_ref[...] = total.reshape(16, 32, 32)

    def right_1():
        gxs[...] = racc[...].astype(BF16).reshape(4, 128, N)
        scatter(gxs, gxr, 0, x_peer, xx)

    def right_2():
        scatter_wait(gxs, gxr, 0)
        own = racc[pl.ds(pl.multiple_of(xx * 128, 128), 128), :]
        for i in range(1, 4):
            own = own + gxr[lax.rem(xx + i, 4)].astype(F32)
        racc[0:128, :] = own
        gys[...] = own.astype(BF16).reshape(4, 32, N)
        scatter(gys, gyr, 1, yl_peer, yl)

    def right_3():
        scatter_wait(gys, gyr, 1)
        own = racc[pl.ds(pl.multiple_of(yl * 32, 32), 32), :]
        for i in range(1, 4):
            own = own + gyr[lax.rem(yl + i, 4)].astype(F32)
        fin[xx, yl] = (own * (1.0 / 128.0)).astype(BF16)
        spread(fin.at[xx], 2, yl_peer, yl, 4)

    def right_4():
        spread_wait(fin.at[xx], 2, 4)
        spread(fin, 3, x_peer, xx, 4)

    def right_5():
        spread_wait(fin, 3, 4)

        def step(j, _):
            dr_ref[j % 8, j // 8] = fin[j // 4, j % 4].astype(F32)
            return 0

        lax.fori_loop(0, 16, step, 0)

    def gate_1(g):
        spread(ga.at[g], 4 + g, zc_peer, me, 16)

    def gate_2(g):
        spread_wait(ga.at[g], 4 + g, 16)
        gc[g, ring] = ga[g].sum(axis=0)
        spread(gc.at[g], 6 + g, y_peer, ring, 8)

    def gate_3(g):
        spread_wait(gc.at[g], 6 + g, 8)
        gb[g, xx] = gc[g].sum(axis=0)
        spread(gb.at[g], 8 + g, x_peer, xx, 4)

    def gate_4(g, out_ref):
        spread_wait(gb.at[g], 8 + g, 4)
        total = gb[g].sum(axis=0) * (1.0 / 512.0)
        for k in range(K):
            out_ref[:, k * CH : (k + 1) * CH] = total[k]

    for copy in load_small():
        copy.wait()
    load_x(0).wait()
    load_c(0).wait()
    make_dmon(0, oth, False)
    pl.semaphore_wait(barrier, 25)
    y_copy(0).start()
    make_dmon(0, yh, True)
    z_send(0, yh)
    for k in range(1, K):
        load_x(k).wait()
        load_c(k).wait()
        make_dmon(k, oth, False)
        y_copy(k).start()
        make_dmon(k, yh, True)
        z_send(k, yh)

    handlers = {DMON: on_dmon, DMIX: on_dmix, MIX: on_mix, MON: on_mon}

    def slot(array, k):
        y_arrived(array * K + k)
        z_send(array * K + k, oth)

    def done(array, k):
        z_arrived(array * K + k)
        handlers[array](k)

    def loop(first, end, body):
        def step(k, _):
            body(k)
            return 0

        lax.fori_loop(first, end, step, 0)

    for k in range(2):
        slot(DMON, k)
    for h in range(2):
        load_r(h).wait()
    build_left()
    lacc[...] = jnp.zeros_like(lacc)
    racc[...] = jnp.zeros_like(racc)
    for k in range(2):
        make_mix(k)

    def dmon_slot(k):
        slot(DMON, k)
        make_mix(k)
        done(DMON, k - 2)

    def dmix_slot(k):
        slot(DMIX, k)
        z_send(MIX * K + k, yh)
        y_copy(MIX * K + k - 2).start()
        done(DMIX, k - 2)

    def mix_slot(k):
        slot(MIX, k)
        done(MIX, k - 2)

    loop(2, K, dmon_slot)
    for k in range(2):
        slot(DMIX, k)
        z_send(MIX * K + k, yh)
        done(DMON, K - 2 + k)
    loop(2, K, dmix_slot)
    for k in range(2):
        slot(MIX, k)
        y_copy(MIX * K + K - 2 + k).start()
        done(DMIX, K - 2 + k)
    right_1()
    gate_1(0)
    loop(2, K - 2, mix_slot)
    right_2()
    gate_2(0)
    loop(K - 2, K, mix_slot)
    for k in range(2):
        slot(MON, k)
        done(MIX, K - 2 + k)
    left_1()
    for k in range(2, K - 2):
        slot(MON, k)
        done(MON, k - 2)
        if k == 4:
            left_2()
    slot(MON, K - 2)
    slot(MON, K - 1)
    right_3()
    gate_3(0)
    done(MON, K - 4)
    done(MON, K - 3)
    right_4()
    left_3()
    done(MON, K - 2)
    gate_4(0, dgi_ref)
    done(MON, K - 1)
    gate_1(1)
    gate_2(1)
    gate_3(1)
    right_5()
    left_out()
    last = 4 * K
    lax.fori_loop(0, last, sends_done, 0)
    gate_4(1, dgo_ref)


def copy_kernel(*refs):
    n = len(refs) // 2
    sem = refs[-1]
    copies = [pltpu.make_async_copy(refs[i], refs[n + i], sem.at[i]) for i in range(n)]
    for copy in copies:
        copy.start()
    for copy in copies:
        copy.wait()


def on_device(inputs, cotangent, block_right, block_left, gate_in, gate_out):
    hbm = pl.BlockSpec(memory_space=pltpu.HBM)
    vmem = pl.BlockSpec(memory_space=pltpu.VMEM)
    sub = 4 * K
    scratch = [
        pltpu.VMEM((16, 32, 32), BF16),
        pltpu.VMEM((1, D), F32),
        pltpu.VMEM((1, D), F32),
        pltpu.VMEM((K, N, CH), BF16),
        pltpu.VMEM((K, N, CH), BF16),
        pltpu.VMEM((K, N, CH), BF16),
        pltpu.VMEM((K, N, CH), F32),
        pltpu.VMEM((K, N, CH), F32),
        pltpu.VMEM((2, 8, 32, N), BF16),
        pltpu.VMEM((N, N), BF16),
        pltpu.VMEM((2, 256, N), BF16),
        pltpu.VMEM((2, 256, N), BF16),
        pltpu.VMEM((sub, 16, 16, CH), BF16),
        pltpu.VMEM((sub, 2, 16, 16, CH), BF16),
        pltpu.VMEM((sub, 2, 16, 16, CH), BF16),
        pltpu.VMEM((N, N), F32),
        pltpu.VMEM((N, N), F32),
        pltpu.VMEM((4, 128, N), BF16),
        pltpu.VMEM((4, 128, N), BF16),
        pltpu.VMEM((4, 32, N), BF16),
        pltpu.VMEM((4, 32, N), BF16),
        pltpu.VMEM((4, 4, 32, N), BF16),
        pltpu.VMEM((4, 8, N), F32),
        pltpu.VMEM((4, 8, N), F32),
        pltpu.VMEM((4, 8, N), F32),
        pltpu.VMEM((4, 8, N), F32),
        pltpu.VMEM((2, 16, K, 1, CH), F32),
        pltpu.VMEM((2, 4, K, 1, CH), F32),
        pltpu.VMEM((2, 8, K, 1, CH), F32),
        pltpu.SemaphoreType.DMA((2 * K + 5,)),
        pltpu.SemaphoreType.DMA((sub,)),
        pltpu.SemaphoreType.DMA((sub,)),
        pltpu.SemaphoreType.DMA((sub,)),
        pltpu.SemaphoreType.DMA((sub,)),
        pltpu.SemaphoreType.DMA((3,)),
        pltpu.SemaphoreType.DMA((3,)),
        pltpu.SemaphoreType.DMA((10,)),
        pltpu.SemaphoreType.DMA((10,)),
    ]
    shapes = (
        ((1, N, D), BF16),
        ((8, 2, 32, N), F32),
        ((16, 32, 32), F32),
        ((1, D), F32),
        ((1, D), F32),
    )
    results = pl.pallas_call(
        kernel,
        out_shape=tuple(pltpu.VMEM(*shape) for shape in shapes),
        in_specs=[hbm] * 6,
        out_specs=(vmem,) * 5,
        scratch_shapes=scratch,
        compiler_params=pltpu.CompilerParams(
            collective_id=0, has_side_effects=True, vmem_limit_bytes=50 * 1024 * 1024
        ),
        name="monarch",
    )(
        *(
            pltpu.with_memory_space_constraint(a, pltpu.HBM)
            for a in (
                inputs,
                cotangent,
                block_right.reshape(8, 2, 32, N),
                block_left,
                gate_in.reshape(1, D),
                gate_out.reshape(1, D),
            )
        )
    )
    d_inputs, d_right, d_left, d_gin, d_gout = pl.pallas_call(
        copy_kernel,
        out_shape=tuple(jax.ShapeDtypeStruct(*shape) for shape in shapes),
        in_specs=[vmem] * 5,
        out_specs=(hbm,) * 5,
        scratch_shapes=[pltpu.SemaphoreType.DMA((5,))],
        name="results",
    )(*(pltpu.with_memory_space_constraint(r, pltpu.VMEM) for r in results))
    return (
        d_inputs,
        d_right.reshape(1, N, N),
        d_left,
        d_gin.reshape(D),
        d_gout.reshape(D),
    )


def solution(mesh):
    in_specs = (
        P("dp", "seq", None),
        P("dp", "seq", None),
        P("seq", None, None),
        P("seq", None, None),
        P(),
        P(),
    )
    out_specs = (P("dp", "seq", None), P("seq", None, None), P("seq", None, None), P(), P())
    return jax.shard_map(
        on_device, mesh=mesh, in_specs=in_specs, out_specs=out_specs, check_vma=False
    )
```
